32 devices in a mesh: groups: 2 (over x), row: 16 (over z, y, core).
Axes of the slice: x: 2, y: 2, z: 4, core: 2. Of those that a mesh axis runs over, the one named last changes fastest.
Arguments:
- features: bfloat16 [8192, 256], P(('groups', 'row')), parts along dimension 0, may hold values from -6 to 6
- self_weight: bfloat16 [256, 256], replicated, may hold values from -0.375 to 0.375
- neigh_weight: bfloat16 [256, 256], replicated, may hold values from -3 to 3
- tile_vals: bfloat16 [64, 64, 128, 128], P(('groups', 'row')), parts along dimension 0, may hold values from 0 to 6, as said below
- tile_cols: int32 [64, 64], P(('groups', 'row')), parts along dimension 0, may hold values from 0 to 31, as said below
- tile_count: int32 [64], P(('groups', 'row')), parts along dimension 0, may hold values from 1 to 64, as said below
- pos_index: int32 [8192], P(('groups', 'row')), parts along dimension 0, may hold values from 0 to 4095
- neg_index: int32 [8192], P(('groups', 'row')), parts along dimension 0, may hold values from 0 to 4095
Outputs:
- loss: float32 [2], P('groups'), parts along dimension 0
- grad_self: float32 [512, 256], P('groups'), parts along dimension 0
- grad_neigh: float32 [512, 256], P('groups'), parts along dimension 0
- grad_feat: float32 [8192, 256], P(('groups', 'row')), parts along dimension 0
The draws below stay inside these ranges and needn't reach their ends.
There are 2 independent parts, one for each index of `groups`. The reference program is written for one: setup_inputs(seed, part) draws one part's arguments, and reference() takes and returns one part's arrays. A program takes and returns all parts, laid end to end along the dimension named above; an argument that names none is the same for every part. Nothing has to cross between parts.
Inputs may be any that keep to these rules, and one draw needn't show every extreme that they name: `tile_vals`: Nonnegative; slot 0 of every row tile has a diagonal of 1 or more. `tile_cols`: slot 0 of row tile r holds column tile r. `tile_count`: some row tile has all 64 slots live.
All inputs are finite; a program needn't handle non-finite values.
Results may differ from the reference program's by a relative error of at most 0.0046.
Values may be sent and summed in bfloat16 or wider, within the bound.
A program may use at most 128 MiB of HBM per device.

```python
import jax
import jax.numpy as jnp
from jax import lax

F = 256
TILE = 128
SLOTS = 64
NODES = 4096
ROW_TILES = 32


def draw_tile_vals(key, part):
    key = jax.random.fold_in(key, 11)
    mask_key, value_key = jax.random.split(key)
    shape = (ROW_TILES, SLOTS, TILE, TILE)
    present = jax.random.bernoulli(mask_key, 0.125, shape).astype(jnp.float32)
    values = jax.random.uniform(value_key, shape, jnp.float32, 0.5, 2.0)
    first_slot = (jnp.arange(SLOTS) == 0).astype(jnp.float32)
    diagonal = first_slot[None, :, None, None] * jnp.eye(TILE, dtype=jnp.float32)[None, None]
    return (present * values + diagonal).astype(jnp.bfloat16)


def draw_tile_cols(key, part):
    key = jax.random.fold_in(key, 12)
    near_key, far_key = jax.random.split(key)
    row_ids = jnp.arange(ROW_TILES, dtype=jnp.int32)[:, None]
    near = (row_ids + jax.random.randint(near_key, (ROW_TILES, SLOTS), -8, 9)) % ROW_TILES
    far = jax.random.randint(far_key, (ROW_TILES, SLOTS), 0, ROW_TILES)
    slot_ids = jnp.arange(SLOTS, dtype=jnp.int32)[None, :]
    picked = jnp.where(slot_ids % 2 == 0, near, far)
    return jnp.where(slot_ids == 0, row_ids, picked).astype(jnp.int32)


def draw_tile_count(key, part):
    key = jax.random.fold_in(key, 13)
    first_key, second_key, full_key = jax.random.split(key, 3)
    first = jax.random.randint(first_key, (ROW_TILES,), 0, SLOTS + 1)
    second = jax.random.randint(second_key, (ROW_TILES,), 0, SLOTS + 1)
    counts = jnp.maximum(1, first * second // SLOTS)
    chosen = jax.random.randint(full_key, (), 0, ROW_TILES)
    return jnp.where(jnp.arange(ROW_TILES) == chosen, SLOTS, counts).astype(jnp.int32)


def place_ends(values, key, low, high):
    shape = values.shape
    spot = [jax.random.randint(jax.random.fold_in(key, axis), (), 0, shape[axis]) for axis in range(len(shape))]
    values = values.at[tuple(spot)].set(low)
    longest = shape.index(max(shape))
    spot[longest] = (spot[longest] + 1) % shape[longest]
    return values.at[tuple(spot)].set(high)


def shard_levels(key, shape, cuts, low, largest):
    level = 1.0
    for dim, shards_of in cuts:
        draws = jax.random.uniform(jax.random.fold_in(jax.random.fold_in(key, 6), dim), (shards_of,), jnp.float32, low / len(cuts), largest / len(cuts))
        level = level * jnp.repeat(jnp.exp(draws), shape[dim] // shards_of).reshape((-1,) + (1,) * (len(shape) - 1 - dim))
    return level


def scatter_about(rng, shape, deviation, most, pieces=(), held_as=jnp.bfloat16):
    drawn = jax.random.normal(rng, shape, jnp.float32) * deviation
    if len(pieces) > 0:
        drawn = shard_levels(rng, shape, pieces, -0.22, 0.18) * drawn
    return jnp.clip(drawn, min=-most, max=most).astype(held_as)


def setup_inputs(seed: int = 0, part: int = 0) -> dict:
    seeds = jax.random.split(jax.random.key(seed), 9)
    own_keys = jax.random.split(jax.random.fold_in(seeds[8], part), 9)
    features = scatter_about(own_keys[0], (NODES, F), 1.0, 6.0, ((0, 16),))
    self_weight = scatter_about(seeds[1], (F, F), F ** -0.5, 0.375)
    neigh_weight = scatter_about(seeds[2], (F, F), 4 ** -0.5, 3.0)
    tile_vals = draw_tile_vals(jax.random.fold_in(jax.random.fold_in(seeds[8], part), 71), part)
    tile_cols = draw_tile_cols(jax.random.fold_in(jax.random.fold_in(seeds[8], part), 71), part)
    tile_count = draw_tile_count(jax.random.fold_in(jax.random.fold_in(seeds[8], part), 71), part)
    pos_index = place_ends(jax.random.randint(own_keys[6], (NODES,), 0, NODES), jax.random.fold_in(own_keys[6], 1), 0, NODES - 1).astype(jnp.int32)
    neg_index = place_ends(jax.random.randint(own_keys[7], (NODES,), 0, NODES), jax.random.fold_in(own_keys[7], 1), 0, NODES - 1).astype(jnp.int32)
    return dict(features=features, self_weight=self_weight, neigh_weight=neigh_weight, tile_vals=tile_vals, tile_cols=tile_cols, tile_count=tile_count, pos_index=pos_index, neg_index=neg_index)


def reference(features, self_weight, neigh_weight, tile_vals, tile_cols, tile_count, pos_index, neg_index):
    node_count = features.shape[0]
    width_f = features.shape[1]
    node_blocks = features.reshape(-1, TILE, width_f)
    live_slot = jnp.arange(SLOTS)[None, :] < tile_count[:, None]
    masked = jnp.where(live_slot[:, :, None, None], tile_vals, jnp.zeros((), tile_vals.dtype))
    degree = lax.optimization_barrier(jnp.sum(masked.astype(jnp.float32), axis=(1, 3)))

    def aggregate(pair):
        values, columns = pair
        picked = node_blocks[columns].astype(jnp.float32)
        return jnp.einsum('sij,sjf->if', values.astype(jnp.float32), picked)
    summed = lax.map(aggregate, (masked, tile_cols))
    mean_near = (summed / degree[:, :, None]).reshape(node_count, width_f).astype(jnp.bfloat16)
    pre = jnp.dot(features, self_weight, preferred_element_type=jnp.float32) + jnp.dot(mean_near, neigh_weight, preferred_element_type=jnp.float32)
    sig_pre = jax.nn.sigmoid(pre)
    hidden = pre * sig_pre
    inverse = 1.0 / jnp.sqrt(lax.optimization_barrier(jnp.sum(hidden * hidden, axis=-1)) + 1e-05)
    embed = hidden * inverse[:, None]
    pos_rows = features[pos_index].astype(jnp.float32)
    neg_rows = features[neg_index].astype(jnp.float32)
    score_pos = lax.optimization_barrier(jnp.sum(embed * pos_rows, axis=-1))
    score_neg = lax.optimization_barrier(jnp.sum(embed * neg_rows, axis=-1))
    loss = jnp.mean(jax.nn.softplus(-score_pos) + jax.nn.softplus(score_neg)).reshape(1)
    d_embed = (-jax.nn.sigmoid(-score_pos))[:, None] * pos_rows + jax.nn.sigmoid(score_neg)[:, None] * neg_rows
    d_hidden = inverse[:, None] * (d_embed - embed * lax.optimization_barrier(jnp.sum(d_embed * embed, axis=-1, keepdims=True)))
    d_pre = (d_hidden * sig_pre * (1.0 + pre * (1.0 - sig_pre))).astype(jnp.bfloat16)
    scale = 1.0 / jnp.sqrt(jnp.float32(node_count))
    grad_self = scale * jnp.dot(features.T, d_pre, preferred_element_type=jnp.float32)
    grad_neigh = scale * jnp.dot(mean_near.T, d_pre, preferred_element_type=jnp.float32)
    degree_rows = degree.reshape(node_count)
    g_neigh = (jnp.dot(d_pre, neigh_weight.T, preferred_element_type=jnp.float32) / degree_rows[:, None]).astype(jnp.bfloat16)

    def spread(total, triple):
        values, columns, g_block = triple
        part = jnp.einsum('sij,if->sjf', values.astype(jnp.float32), g_block.astype(jnp.float32))
        return (total.at[columns].add(part), None)
    start_total = jnp.zeros((ROW_TILES, TILE, width_f), jnp.float32)
    spread_total, _ = lax.scan(spread, start_total, (masked, tile_cols, g_neigh.reshape(-1, TILE, width_f)))
    grad_feat = jnp.dot(d_pre, self_weight.T, preferred_element_type=jnp.float32) + spread_total.reshape(node_count, width_f)
    return (loss, grad_self, grad_neigh, grad_feat)
```

```python
import functools

import jax
import jax.numpy as jnp
from jax import lax
from jax.experimental import pallas as pl
from jax.experimental.pallas import tpu as pltpu
from jax.sharding import PartitionSpec as P

F32 = jnp.float32
BF16 = jnp.bfloat16
MESH = pl.DeviceIdType.MESH
SLOT_BLOCK = 16


def dense_kernel(cols_ref, count_ref, tiles_ref, adj_ref, deg_ref, acc):
    r, b = pl.program_id(0), pl.program_id(1)
    block = tiles_ref.shape[1]
    column_tiles, tile, _ = acc.shape

    @pl.when(b == 0)
    def _():
        def clear(i, carry):
            acc[i] = jnp.zeros((tile, tile), F32)
            return carry

        lax.fori_loop(0, column_tiles, clear, 0)

    live = jnp.clip(count_ref[r] - b * block, 0, block)

    def add(i, carry):
        col = cols_ref[r, b * block + i]
        acc[col] += tiles_ref[0, i].astype(F32)
        return carry

    lax.fori_loop(0, live, add, 0)

    @pl.when(b == pl.num_programs(1) - 1)
    def _():
        def finish(p, total):
            left, right = acc[2 * p], acc[2 * p + 1]
            adj_ref[p, :, :tile] = left.astype(BF16)
            adj_ref[p, :, tile:] = right.astype(BF16)
            return total + left + right

        total = lax.fori_loop(0, column_tiles // 2, finish, jnp.zeros((tile, tile), F32))
        deg_ref[...] = jnp.broadcast_to(jnp.sum(total, axis=1, keepdims=True), (tile, tile))


def dense_rows(tile_vals, tile_cols, tile_count, shards):
    tile_rows, slots, tile, _ = tile_vals.shape
    block = SLOT_BLOCK if slots % SLOT_BLOCK == 0 else slots

    def tiles_at(r, b, cols, count):
        return (r, jnp.minimum(b, (count[r] - 1) // block), 0, 0)

    return pl.pallas_call(
        dense_kernel,
        grid_spec=pltpu.PrefetchScalarGridSpec(
            num_scalar_prefetch=2,
            grid=(tile_rows, slots // block),
            in_specs=[pl.BlockSpec((1, block, tile, tile), tiles_at)],
            out_specs=[
                pl.BlockSpec((shards, tile, 2 * tile), lambda r, b, cols, count: (0, r, 0)),
                pl.BlockSpec((tile, tile), lambda r, b, cols, count: (r, 0)),
            ],
            scratch_shapes=[pltpu.VMEM((2 * shards, tile, tile), F32)],
        ),
        out_shape=[
            jax.ShapeDtypeStruct((shards, tile_rows * tile, 2 * tile), BF16),
            jax.ShapeDtypeStruct((tile_rows * tile, tile), F32),
        ],
        compiler_params=pltpu.CompilerParams(vmem_limit_bytes=48 * 1024 * 1024),
    )(tile_cols, tile_count, tile_vals)


def layer_kernel(
    Z, x_ref, ws_ref, wn_ref, adj_ref, deg_ref, pos_ref, neg_ref,
    loss_ref, gself_ref, gneigh_ref, gfeat_ref,
    feats, adj, adj_p, idx, acc, dpre, mean,
    gnt, gn32, gfull, g_in, gy_out, gy_in, gz, gh, gp,
    l_own, l_core, l_sum, l_y, lz,
    y_out, y_in, z_out, up_in, dn_in,
    adj_sem, adjp_s, adjp_r, recv, up_s, dn_s, y_s, core_s,
    ex_s, ex_r, gz_s, gz_r, lz_s, lz_r, ys_s, ys_r, zs_s, up_r, dn_r,
):
    rows, width = x_ref.shape
    half = rows // 2
    me = lax.axis_index("row")
    z, y, c = me // 4, (me // 2) % 2, me % 2

    def dev(zz, yy, cc):
        return (zz * 2 + yy) * 2 + cc

    core_peer, y_peer = dev(z, y, 1 - c), dev(z, 1 - y, c)
    up_peer = dev(jnp.minimum(z + 1, Z - 1), y, c)
    dn_peer = dev(jnp.maximum(z - 1, 0), y, c)

    def remote(src, dst, ss, rs, target):
        return pltpu.make_async_remote_copy(
            src_ref=src, dst_ref=dst, send_sem=ss, recv_sem=rs,
            device_id={"row": target}, device_id_type=MESH,
        )

    adj_load = pltpu.make_async_copy(adj_ref, adj, adj_sem)
    adj_load.start()

    barrier = pltpu.get_barrier_semaphore()
    pl.semaphore_signal(barrier, inc=1, device_id={"row": core_peer}, device_id_type=MESH)
    pl.semaphore_signal(barrier, inc=1, device_id={"row": y_peer}, device_id_type=MESH)
    for k in range(1, Z):
        pl.semaphore_signal(
            barrier, inc=1, device_id={"row": dev((z + k) % Z, y, c)}, device_id_type=MESH
        )
    feats[me] = x_ref[...]
    pl.semaphore_wait(barrier, Z + 1)

    def go_up(zs):
        s = dev(zs, y, c)
        return remote(feats.at[s], feats.at[s], up_s.at[zs], recv.at[s], up_peer)

    def go_dn(zs):
        s = dev(zs, y, c)
        return remote(feats.at[s], feats.at[s], dn_s.at[zs], recv.at[s], dn_peer)

    def go_y(zs):
        s = dev(zs, y, c)
        return remote(feats.at[s], feats.at[s], y_s.at[zs], recv.at[s], y_peer)

    def go_core(zs, yy):
        s = dev(zs, yy, c)
        return remote(feats.at[s], feats.at[s], core_s.at[zs * 2 + yy], recv.at[s], core_peer)

    def arrived(s):
        remote(feats.at[s], feats.at[s], core_s.at[0], recv.at[s], core_peer).wait_recv()

    @pl.when(z < Z - 1)
    def _():
        go_up(z).start()

    @pl.when(z > 0)
    def _():
        go_dn(z).start()

    go_y(z).start()
    go_core(z, y).start()
    adj_swap = remote(adj_ref.at[:, 1 - c], adj_p, adjp_s, adjp_r, core_peer)

    idx[:rows] = jnp.transpose(jnp.broadcast_to(pos_ref[...], (128, rows)))
    idx[rows:] = jnp.transpose(jnp.broadcast_to(neg_ref[...], (128, rows)))
    acc[...] = jnp.zeros_like(acc)
    adj_load.wait()
    adj_swap.start()

    def use(s):
        block = feats[s]
        acc[:rows] += jnp.dot(adj[s // 2, s % 2], block, preferred_element_type=F32)
        lane = lax.broadcasted_iota(jnp.int32, (2 * rows, 128), 1) + s * rows
        parts = [
            jnp.where(idx[...] == lane + o, 1.0, 0.0).astype(BF16) for o in range(0, rows, 128)
        ]
        acc[rows:] += jnp.dot(
            jnp.concatenate(parts, axis=1), block, preferred_element_type=F32
        )

    use(me)

    def at(d, sign):
        zs = z + sign * d
        ok = (zs >= 0) & (zs < Z) & (d >= 0)
        return zs, (ok & (d > 0)) if sign > 0 else ok

    def gather_step(k, carry):
        zs, ok = at(k, -1)

        @pl.when(ok)
        def _():
            arrived(dev(zs, y, c))

            @pl.when(z < Z - 1)
            def _():
                go_up(zs).start()

            go_y(zs).start()
            go_core(zs, y).start()

        zt, okt = at(k, 1)

        @pl.when(okt)
        def _():
            arrived(dev(zt, y, c))

            @pl.when(z > 0)
            def _():
                go_dn(zt).start()

            go_y(zt).start()
            go_core(zt, y).start()

        for sign in (-1, 1):
            zy, oky = at(k - 1, sign)

            @pl.when(oky)
            def _():
                arrived(dev(zy, 1 - y, c))
                go_core(zy, 1 - y).start()

        def use_at(d, sign, yy, cc, wait):
            zu, oku = at(d, sign)

            @pl.when(oku)
            def _():
                s = dev(zu, yy, cc)
                if wait:
                    arrived(s)
                use(s)

        for sign in (-1, 1):
            use_at(k, sign, y, c, False)
            use_at(k - 1, sign, 1 - y, c, False)
            use_at(k - 1, sign, y, 1 - c, True)
            use_at(k - 2, sign, 1 - y, 1 - c, True)
        return carry

    lax.fori_loop(1, Z + 2, gather_step, 0)

    step = 64

    def rows_step(i, total):
        at_rows = pl.ds(pl.multiple_of(i * step, step), step)
        dg = jnp.concatenate([deg_ref[at_rows]] * (width // 128), axis=1)
        near = (acc[at_rows] / dg).astype(BF16)
        mean[at_rows] = near
        pre = jnp.dot(x_ref[at_rows], ws_ref[...], preferred_element_type=F32) + jnp.dot(
            near, wn_ref[...], preferred_element_type=F32
        )
        sig = jax.nn.sigmoid(pre)
        hid = pre * sig
        inv = 1.0 / jnp.sqrt(jnp.sum(hid * hid, axis=-1, keepdims=True) + 1e-05)
        emb = hid * inv
        pos = acc[pl.ds(pl.multiple_of(rows + i * step, step), step)]
        neg = acc[pl.ds(pl.multiple_of(2 * rows + i * step, step), step)]
        a = jnp.sum(emb * pos, axis=-1, keepdims=True)
        b = jnp.sum(emb * neg, axis=-1, keepdims=True)
        part = (
            jnp.maximum(-a, 0.0) + jnp.log1p(jnp.exp(-jnp.abs(a)))
            + jnp.maximum(b, 0.0) + jnp.log1p(jnp.exp(-jnp.abs(b)))
        )
        demb = -jax.nn.sigmoid(-a) * pos + jax.nn.sigmoid(b) * neg
        dhid = inv * (demb - emb * jnp.sum(demb * emb, axis=-1, keepdims=True))
        dp = (dhid * sig * (1.0 + pre * (1.0 - sig))).astype(BF16)
        dpre[at_rows] = dp
        gn32[at_rows] = (
            lax.dot_general(dp, wn_ref[...], (((1,), (1,)), ((), ())), preferred_element_type=F32)
            / dg
        )
        return total + jnp.sum(part, axis=0, keepdims=True)

    total = lax.fori_loop(0, rows // step, rows_step, jnp.zeros((1, 1), F32))
    gnt[0] = jnp.transpose(gn32[...]).astype(BF16)
    ex_gn = remote(gnt.at[0], gnt.at[1], ex_s.at[0], ex_r.at[0], core_peer)
    ex_gn.start()
    l_own[...] = jnp.broadcast_to(total, l_own.shape)
    ex_l = remote(l_own, l_core, ex_s.at[1], ex_r.at[1], core_peer)
    ex_l.start()

    scale = 1.0 / jnp.sqrt(F32(Z * 4 * rows))
    contract0 = (((0,), (0,)), ((), ()))
    gfull[0] = scale * lax.dot_general(x_ref[...], dpre[...], contract0, preferred_element_type=F32)
    gfull[1] = scale * lax.dot_general(mean[...], dpre[...], contract0, preferred_element_type=F32)
    ex_g = remote(gfull.at[1 - c], g_in, ex_s.at[2], ex_r.at[2], core_peer)
    ex_g.start()

    adj_swap.wait_recv()
    ex_gn.wait_recv()
    low = (z * 2) // Z

    def dest(j):
        return low * j + (1 - low) * (Z - 1 - j)

    def spread(zd, yd):
        return jnp.dot(gnt[0], adj[zd * 2 + yd, c], preferred_element_type=F32) + jnp.dot(
            gnt[1], adj_p[zd * 2 + yd], preferred_element_type=F32
        )

    def y_copy(zd):
        return remote(y_out.at[zd], y_in.at[zd], ys_s.at[zd], ys_r.at[zd], y_peer)

    def y_step(j, carry):
        zd = dest(j)
        y_out[zd] = spread(zd, 1 - y).astype(BF16)
        y_copy(zd).start()
        return carry

    lax.fori_loop(0, Z // 2, y_step, 0)

    ex_l.wait_recv()
    l_sum[...] = l_own[...] + l_core[...]
    ex_ly = remote(l_sum, l_y, ex_s.at[3], ex_r.at[3], y_peer)
    ex_ly.start()
    ex_g.wait_recv()
    other = pl.ds(pl.multiple_of((1 - y) * half, half), half)
    own = pl.ds(pl.multiple_of(y * half, half), half)
    gy_out[...] = (gfull[c, other] + g_in[other]).astype(BF16)
    ex_gy = remote(gy_out, gy_in, ex_s.at[4], ex_r.at[4], y_peer)
    ex_gy.start()

    lax.fori_loop(Z // 2, Z, y_step, 0)

    def up_copy(zd):
        return remote(z_out.at[zd], up_in.at[zd], zs_s.at[zd], up_r.at[zd], up_peer)

    def dn_copy(zd):
        return remote(z_out.at[zd], dn_in.at[zd], zs_s.at[zd], dn_r.at[zd], dn_peer)

    def z_step(j, carry):
        zd = dest(j)
        mine = spread(zd, y)
        y_copy(zd).wait_recv()
        gn32[...] = mine + y_in[zd].astype(F32)

        @pl.when(zd > z)
        def _():
            @pl.when(z > 0)
            def _():
                up_copy(zd).wait_recv()
                gn32[...] += up_in[zd].astype(F32)

            z_out[zd] = gn32[...].astype(BF16)
            up_copy(zd).start()

        @pl.when(zd < z)
        def _():
            @pl.when(z < Z - 1)
            def _():
                dn_copy(zd).wait_recv()
                gn32[...] += dn_in[zd].astype(F32)

            z_out[zd] = gn32[...].astype(BF16)
            dn_copy(zd).start()

        @pl.when(zd == z)
        def _():
            acc[:rows] = gn32[...]

        return carry

    lax.fori_loop(0, 1, z_step, 0)

    ex_ly.wait_recv()
    ex_gy.wait_recv()
    lz[z] = l_sum[...] + l_y[...]
    gz[z] = (gfull[c, own] + g_in[own] + gy_in[...].astype(F32)).astype(BF16)

    def gz_copy(k, slot):
        return remote(gz.at[slot], gz.at[slot], gz_s.at[k], gz_r.at[slot], dev((z + k) % Z, y, c))

    def lz_copy(k, slot):
        return remote(lz.at[slot], lz.at[slot], lz_s.at[k], lz_r.at[slot], dev((z + k) % Z, y, c))

    def gz_start(k, carry):
        gz_copy(k, z).start()
        lz_copy(k, z).start()
        return carry

    lax.fori_loop(1, Z, gz_start, 0)

    lax.fori_loop(1, Z, z_step, 0)

    def gz_wait(k, carry):
        slot = (z + k) % Z
        gz_copy(k, slot).wait_recv()
        lz_copy(k, slot).wait_recv()
        return carry

    lax.fori_loop(1, Z, gz_wait, 0)
    g_total, l_total = gz[0].astype(F32), lz[0]
    for k in range(1, Z):
        g_total = g_total + gz[k].astype(F32)
        l_total = l_total + lz[k]
    gh[y] = g_total.astype(BF16)
    ex_gh = remote(gh.at[y], gh.at[y], ex_s.at[5], ex_r.at[5], y_peer)
    ex_gh.start()
    loss_ref[...] = l_total / F32(Z * 4 * rows)

    direct = lax.dot_general(
        dpre[...], ws_ref[...], (((1,), (1,)), ((), ())), preferred_element_type=F32
    )

    @pl.when(z > 0)
    def _():
        up_copy(z).wait_recv()
        acc[:rows] += up_in[z].astype(F32)

    @pl.when(z < Z - 1)
    def _():
        dn_copy(z).wait_recv()
        acc[:rows] += dn_in[z].astype(F32)

    remote(gh.at[1 - y], gh.at[1 - y], ex_s.at[5], ex_r.at[5], y_peer).wait_recv()
    ex_gp = remote(gh, gp, ex_s.at[6], ex_r.at[6], core_peer)
    ex_gp.start()
    gfeat_ref[...] = direct + jnp.transpose(acc[:rows])
    ex_gp.wait_recv()

    @pl.when(c == 0)
    def _():
        for h in range(2):
            gself_ref[h * half : (h + 1) * half] = gh[h].astype(F32)
            gneigh_ref[h * half : (h + 1) * half] = gp[h].astype(F32)

    @pl.when(c == 1)
    def _():
        for h in range(2):
            gself_ref[h * half : (h + 1) * half] = gp[h].astype(F32)
            gneigh_ref[h * half : (h + 1) * half] = gh[h].astype(F32)

    def sent(zs, carry):
        @pl.when((zs <= z) & (z < Z - 1))
        def _():
            go_up(zs).wait_send()

        @pl.when((zs >= z) & (z > 0))
        def _():
            go_dn(zs).wait_send()

        go_y(zs).wait_send()
        go_core(zs, 0).wait_send()
        go_core(zs, 1).wait_send()
        y_copy(zs).wait_send()

        @pl.when(zs != z)
        def _():
            up_copy(zs).wait_send()

        return carry

    lax.fori_loop(0, Z, sent, 0)

    def sent_z(k, carry):
        gz_copy(k, z).wait_send()
        lz_copy(k, z).wait_send()
        return carry

    lax.fori_loop(1, Z, sent_z, 0)
    for copy in (adj_swap, ex_gn, ex_l, ex_g, ex_ly, ex_gy, ex_gh, ex_gp):
        copy.wait_send()


def on_device(
    features, self_weight, neigh_weight, tile_vals, tile_cols, tile_count, pos_index, neg_index
):
    rows, width = features.shape
    shards = lax.axis_size("row")
    Z = shards // 4
    adj, degree = dense_rows(tile_vals, tile_cols, tile_count, shards)
    adj = adj.reshape(shards // 2, 2, rows, rows)
    vmem = pl.BlockSpec(memory_space=pltpu.VMEM)
    half = rows // 2
    dma = pltpu.SemaphoreType.DMA
    loss, grad_self, grad_neigh, grad_feat = pl.pallas_call(
        functools.partial(layer_kernel, Z),
        in_specs=[vmem, vmem, vmem, pl.BlockSpec(memory_space=pl.ANY), vmem, vmem, vmem],
        out_specs=[vmem] * 4,
        out_shape=[
            jax.ShapeDtypeStruct((8, 128), F32),
            jax.ShapeDtypeStruct((width, width), F32),
            jax.ShapeDtypeStruct((width, width), F32),
            jax.ShapeDtypeStruct((rows, width), F32),
        ],
        scratch_shapes=[
            pltpu.VMEM((shards, rows, width), BF16),
            pltpu.VMEM((shards // 2, 2, rows, rows), BF16),
            pltpu.VMEM((shards // 2, rows, rows), BF16),
            pltpu.VMEM((2 * rows, 128), jnp.int32),
            pltpu.VMEM((3 * rows, width), F32),
            pltpu.VMEM((rows, width), BF16),
            pltpu.VMEM((rows, width), BF16),
            pltpu.VMEM((2, width, rows), BF16),
            pltpu.VMEM((rows, width), F32),
            pltpu.VMEM((2, width, width), F32),
            pltpu.VMEM((width, width), F32),
            pltpu.VMEM((half, width), BF16),
            pltpu.VMEM((half, width), BF16),
            pltpu.VMEM((Z, half, width), BF16),
            pltpu.VMEM((2, half, width), BF16),
            pltpu.VMEM((2, half, width), BF16),
            pltpu.VMEM((8, 128), F32),
            pltpu.VMEM((8, 128), F32),
            pltpu.VMEM((8, 128), F32),
            pltpu.VMEM((8, 128), F32),
            pltpu.VMEM((Z, 8, 128), F32),
            pltpu.VMEM((Z, width, rows), BF16),
            pltpu.VMEM((Z, width, rows), BF16),
            pltpu.VMEM((Z, width, rows), BF16),
            pltpu.VMEM((Z, width, rows), BF16),
            pltpu.VMEM((Z, width, rows), BF16),
            dma(()), dma(()), dma(()), dma((shards,)), dma((Z,)), dma((Z,)), dma((Z,)),
            dma((2 * Z,)), dma((7,)), dma((7,)), dma((Z,)), dma((Z,)), dma((Z,)), dma((Z,)),
            dma((Z,)), dma((Z,)), dma((Z,)), dma((Z,)), dma((Z,)),
        ],
        compiler_params=pltpu.CompilerParams(
            collective_id=0, has_side_effects=True, vmem_limit_bytes=56 * 1024 * 1024
        ),
    )(
        features, self_weight, neigh_weight, adj, degree,
        pos_index.reshape(1, rows), neg_index.reshape(1, rows),
    )
    return (loss[0, :1], grad_self, grad_neigh, grad_feat)


def solution(mesh):
    placed = (
        P(("groups", "row"), None),
        P(),
        P(),
        P(("groups", "row"), None, None, None),
        P(("groups", "row"), None),
        P(("groups", "row")),
        P(("groups", "row")),
        P(("groups", "row")),
    )
    return jax.shard_map(
        on_device,
        mesh=mesh,
        in_specs=placed,
        out_specs=(P("groups"), P("groups", None), P("groups", None), P(("groups", "row"), None)),
        check_vma=False,
    )
```

```python
import functools

import jax
import jax.numpy as jnp
from jax import lax
from jax.experimental import pallas as pl
from jax.experimental.pallas import tpu as pltpu
from jax.sharding import PartitionSpec as P

F32 = jnp.float32
BF16 = jnp.bfloat16
MESH = pl.DeviceIdType.MESH
SLOT_BLOCK = 16


def dense_kernel(cols_ref, count_ref, tiles_ref, adj_ref, deg_ref, acc):
    r, b = pl.program_id(0), pl.program_id(1)
    block = tiles_ref.shape[1]
    column_tiles, tile, _ = acc.shape

    @pl.when(b == 0)
    def _():
        def clear(i, carry):
            acc[i] = jnp.zeros((tile, tile), F32)
            return carry

        lax.fori_loop(0, column_tiles, clear, 0)

    live = jnp.clip(count_ref[r] - b * block, 0, block)

    def add(i, carry):
        col = cols_ref[r, b * block + i]
        acc[col] += tiles_ref[0, i].astype(F32)
        return carry

    lax.fori_loop(0, live, add, 0)

    @pl.when(b == pl.num_programs(1) - 1)
    def _():
        def finish(p, total):
            left, right = acc[2 * p], acc[2 * p + 1]
            adj_ref[p, :, :tile] = left.astype(BF16)
            adj_ref[p, :, tile:] = right.astype(BF16)
            return total + left + right

        total = lax.fori_loop(0, column_tiles // 2, finish, jnp.zeros((tile, tile), F32))
        deg_ref[...] = jnp.broadcast_to(jnp.sum(total, axis=1, keepdims=True), (tile, tile))


def dense_rows(tile_vals, tile_cols, tile_count, shards):
    tile_rows, slots, tile, _ = tile_vals.shape
    block = SLOT_BLOCK if slots % SLOT_BLOCK == 0 else slots

    def tiles_at(r, b, cols, count):
        return (r, jnp.minimum(b, (count[r] - 1) // block), 0, 0)

    return pl.pallas_call(
        dense_kernel,
        grid_spec=pltpu.PrefetchScalarGridSpec(
            num_scalar_prefetch=2,
            grid=(tile_rows, slots // block),
            in_specs=[pl.BlockSpec((1, block, tile, tile), tiles_at)],
            out_specs=[
                pl.BlockSpec((shards, tile, 2 * tile), lambda r, b, cols, count: (0, r, 0)),
                pl.BlockSpec((tile, tile), lambda r, b, cols, count: (r, 0)),
            ],
            scratch_shapes=[pltpu.VMEM((2 * shards, tile, tile), F32)],
        ),
        out_shape=[
            jax.ShapeDtypeStruct((shards, tile_rows * tile, 2 * tile), BF16),
            jax.ShapeDtypeStruct((tile_rows * tile, tile), F32),
        ],
        compiler_params=pltpu.CompilerParams(
            vmem_limit_bytes=48 * 1024 * 1024
        ),
    )(tile_cols, tile_count, tile_vals)


def layer_kernel(
    Z, x_hbm, ws_hbm, wn_hbm, adj, deg_hbm, pos_ref, neg_ref,
    loss_ref, grads_ref, gfeat_ref,
    feats, ws, wn, deg, adj_p, idx, acc, dpre, mean,
    gnt, gn32, gfull, g_in, gy_out, gy_in, gz, gh, gp,
    l_own, l_core, l_sum, l_y, lz,
    y_out, y_in, z_out, up_in, dn_in, tsum, town,
    load_sem, adjp_s, adjp_r, recv, up_s, dn_s, y_s, core_s,
    ex_s, ex_r, gz_s, gz_r, lz_s, lz_r, ys_s, ys_r, zs_s, up_r, dn_r,
):
    rows, width = x_hbm.shape
    half = rows // 2
    me = lax.axis_index("row")
    z, y, c = me // 4, (me // 2) % 2, me % 2

    def dev(zz, yy, cc):
        return (zz * 2 + yy) * 2 + cc

    core_peer, y_peer = dev(z, y, 1 - c), dev(z, 1 - y, c)
    up_peer = dev(jnp.minimum(z + 1, Z - 1), y, c)
    dn_peer = dev(jnp.maximum(z - 1, 0), y, c)

    def remote(src, dst, ss, rs, target):
        return pltpu.make_async_remote_copy(
            src_ref=src, dst_ref=dst, send_sem=ss, recv_sem=rs,
            device_id={"row": target}, device_id_type=MESH,
        )

    loads = [
        pltpu.make_async_copy(x_hbm, feats.at[me], load_sem.at[0]),
        pltpu.make_async_copy(ws_hbm, ws, load_sem.at[1]),
        pltpu.make_async_copy(wn_hbm, wn, load_sem.at[2]),
        pltpu.make_async_copy(deg_hbm, deg, load_sem.at[3]),
    ]
    loads[0].start()
    for load in loads[1:]:
        load.start()

    barrier = pltpu.get_barrier_semaphore()
    pl.semaphore_signal(barrier, inc=1, device_id={"row": core_peer}, device_id_type=MESH)
    pl.semaphore_signal(barrier, inc=1, device_id={"row": y_peer}, device_id_type=MESH)
    for k in range(1, Z):
        pl.semaphore_signal(
            barrier, inc=1, device_id={"row": dev((z + k) % Z, y, c)}, device_id_type=MESH
        )
    loads[0].wait()
    pl.semaphore_wait(barrier, Z + 1)

    def part(s, h):
        return feats.at[s, pl.ds(h * half, half)]

    def hop(s, h, sem, target):
        return remote(part(s, h), part(s, h), sem, recv.at[2 * s + h], target)

    def go_up(zs, h):
        return hop(dev(zs, y, c), h, up_s.at[2 * zs + h], up_peer)

    def go_dn(zs, h):
        return hop(dev(zs, y, c), h, dn_s.at[2 * zs + h], dn_peer)

    def go_y(zs, h):
        return hop(dev(zs, y, c), h, y_s.at[2 * zs + h], y_peer)

    def go_core(zs, yy, h):
        return hop(dev(zs, yy, c), h, core_s.at[4 * zs + 2 * yy + h], core_peer)

    def arrived(s, h):
        hop(s, h, core_s.at[0], core_peer).wait_recv()

    for h in range(2):
        @pl.when(z < Z - 1)
        def _():
            go_up(z, h).start()

        @pl.when(z > 0)
        def _():
            go_dn(z, h).start()

        go_y(z, h).start()
        go_core(z, y, h).start()

    adj_swap = remote(adj.at[:, 1 - c], adj_p, adjp_s, adjp_r, core_peer)

    idx[:rows] = jnp.transpose(jnp.broadcast_to(pos_ref[...], (128, rows)))
    idx[rows:] = jnp.transpose(jnp.broadcast_to(neg_ref[...], (128, rows)))
    acc[...] = jnp.zeros_like(acc)
    adj_swap.start()

    def use(s):
        block = feats[s]
        acc[:rows] += jnp.dot(adj[s // 2, s % 2], block, preferred_element_type=F32)
        lane = lax.broadcasted_iota(jnp.int32, (2 * rows, 128), 1) + s * rows
        parts = [
            jnp.where(idx[...] == lane + o, 1.0, 0.0).astype(BF16) for o in range(0, rows, 128)
        ]
        acc[rows:] += jnp.dot(
            jnp.concatenate(parts, axis=1), block, preferred_element_type=F32
        )

    use(me)

    def at(d, sign):
        zs = z + sign * d
        ok = (zs >= 0) & (zs < Z) & (d >= 0)
        return zs, (ok & (d > 0)) if sign > 0 else ok

    def gather_step(k, carry):
        for h in range(2):
            zs, ok = at(k, -1)

            @pl.when(ok)
            def _():
                arrived(dev(zs, y, c), h)

                @pl.when(z < Z - 1)
                def _():
                    go_up(zs, h).start()

                go_y(zs, h).start()
                go_core(zs, y, h).start()

            zt, okt = at(k, 1)

            @pl.when(okt)
            def _():
                arrived(dev(zt, y, c), h)

                @pl.when(z > 0)
                def _():
                    go_dn(zt, h).start()

                go_y(zt, h).start()
                go_core(zt, y, h).start()

        for h in range(2):
            for sign in (-1, 1):
                zy, oky = at(k - 1, sign)

                @pl.when(oky)
                def _():
                    arrived(dev(zy, 1 - y, c), h)
                    go_core(zy, 1 - y, h).start()

        def use_at(d, sign, yy, cc, wait):
            zu, oku = at(d, sign)

            @pl.when(oku)
            def _():
                s = dev(zu, yy, cc)
                if wait:
                    arrived(s, 0)
                    arrived(s, 1)
                use(s)

        for sign in (-1, 1):
            use_at(k, sign, y, c, False)
            use_at(k - 1, sign, 1 - y, c, False)
            use_at(k - 1, sign, y, 1 - c, True)
            use_at(k - 2, sign, 1 - y, 1 - c, True)
        return carry

    lax.fori_loop(1, Z + 2, gather_step, 0)

    step = 64
    for load in loads[1:]:
        load.wait()

    def rows_step(i, total):
        at_rows = pl.ds(pl.multiple_of(i * step, step), step)
        dg = jnp.concatenate([deg[at_rows]] * (width // 128), axis=1)
        near = (acc[at_rows] / dg).astype(BF16)
        mean[at_rows] = near
        pre = jnp.dot(feats[me, at_rows], ws[...], preferred_element_type=F32) + jnp.dot(
            near, wn[...], preferred_element_type=F32
        )
        sig = jax.nn.sigmoid(pre)
        hid = pre * sig
        inv = 1.0 / jnp.sqrt(jnp.sum(hid * hid, axis=-1, keepdims=True) + 1e-05)
        emb = hid * inv
        pos = acc[pl.ds(pl.multiple_of(rows + i * step, step), step)]
        neg = acc[pl.ds(pl.multiple_of(2 * rows + i * step, step), step)]
        a = jnp.sum(emb * pos, axis=-1, keepdims=True)
        b = jnp.sum(emb * neg, axis=-1, keepdims=True)
        part = (
            jnp.maximum(-a, 0.0) + jnp.log1p(jnp.exp(-jnp.abs(a)))
            + jnp.maximum(b, 0.0) + jnp.log1p(jnp.exp(-jnp.abs(b)))
        )
        demb = -jax.nn.sigmoid(-a) * pos + jax.nn.sigmoid(b) * neg
        dhid = inv * (demb - emb * jnp.sum(demb * emb, axis=-1, keepdims=True))
        dp = (dhid * sig * (1.0 + pre * (1.0 - sig))).astype(BF16)
        dpre[at_rows] = dp
        gn32[at_rows] = (
            lax.dot_general(dp, wn[...], (((1,), (1,)), ((), ())), preferred_element_type=F32)
            / dg
        )
        return total + jnp.sum(part, axis=0, keepdims=True)

    total = lax.fori_loop(0, rows // step, rows_step, jnp.zeros((1, 1), F32), unroll=True)
    gnt[0] = jnp.transpose(gn32[...]).astype(BF16)
    ex_gn = remote(gnt.at[0], gnt.at[1], ex_s.at[0], ex_r.at[0], core_peer)
    ex_gn.start()
    l_own[...] = jnp.broadcast_to(total, l_own.shape)
    ex_l = remote(l_own, l_core, ex_s.at[1], ex_r.at[1], core_peer)
    ex_l.start()

    scale = 1.0 / jnp.sqrt(F32(Z * 4 * rows))
    contract0 = (((0,), (0,)), ((), ()))
    gfull[0] = scale * lax.dot_general(feats[me], dpre[...], contract0, preferred_element_type=F32)
    gfull[1] = scale * lax.dot_general(mean[...], dpre[...], contract0, preferred_element_type=F32)
    ex_g = remote(gfull.at[1 - c], g_in, ex_s.at[2], ex_r.at[2], core_peer)
    ex_g.start()

    adj_swap.wait_recv()
    ex_gn.wait_recv()
    low = (z * 2) // Z

    def dest(j):
        own_at = low * z + (1 - low) * (Z - 1 - z)
        skip, last = (j + Z - own_at) // Z, (j + 1) // Z
        return last * z + (1 - last) * (low * (j + skip) + (1 - low) * (Z - 1 - j - skip))

    def spread(zd, h, yd):
        at_half = pl.ds(pl.multiple_of(h * half, half), half)
        return jnp.dot(
            gnt[0, at_half], adj[zd * 2 + yd, c], preferred_element_type=F32
        ) + jnp.dot(gnt[1, at_half], adj_p[zd * 2 + yd], preferred_element_type=F32)

    def y_copy(i):
        return remote(y_out.at[i], y_in.at[i], ys_s.at[i], ys_r.at[i], y_peer)

    def y_step(i, carry):
        zd, h = dest(i // 2), i % 2
        slot = 2 * zd + h
        y_out[slot] = spread(zd, h, 1 - y).astype(BF16)
        y_copy(slot).start()
        return carry

    lax.fori_loop(0, 1, y_step, 0)

    ex_l.wait_recv()
    l_sum[...] = l_own[...] + l_core[...]
    ex_ly = remote(l_sum, l_y, ex_s.at[3], ex_r.at[3], y_peer)
    ex_ly.start()
    ex_g.wait_recv()
    other = pl.ds(pl.multiple_of((1 - y) * half, half), half)
    own = pl.ds(pl.multiple_of(y * half, half), half)
    gy_out[...] = (gfull[c, other] + g_in[other]).astype(BF16)
    ex_gy = remote(gy_out, gy_in, ex_s.at[4], ex_r.at[4], y_peer)
    ex_gy.start()

    lax.fori_loop(1, 2 * Z - 2, y_step, 0)

    def up_copy(i):
        return remote(z_out.at[i], up_in.at[i], zs_s.at[i], up_r.at[i], up_peer)

    def dn_copy(i):
        return remote(z_out.at[i], dn_in.at[i], zs_s.at[i], dn_r.at[i], dn_peer)

    def z_step(i, carry):
        zd, h = dest(i // 2), i % 2
        slot = 2 * zd + h
        mine = spread(zd, h, y)
        y_copy(slot).wait_recv()
        tsum[...] = mine + y_in[slot].astype(F32)

        @pl.when(zd > z)
        def _():
            @pl.when(z > 0)
            def _():
                up_copy(slot).wait_recv()
                tsum[...] += up_in[slot].astype(F32)

            z_out[slot] = tsum[...].astype(BF16)
            up_copy(slot).start()

        @pl.when(zd < z)
        def _():
            @pl.when(z < Z - 1)
            def _():
                dn_copy(slot).wait_recv()
                tsum[...] += dn_in[slot].astype(F32)

            z_out[slot] = tsum[...].astype(BF16)
            dn_copy(slot).start()

        @pl.when(zd == z)
        def _():
            town[h] = tsum[...]

        return carry

    lax.fori_loop(0, 1, z_step, 0)

    ex_ly.wait_recv()
    ex_gy.wait_recv()
    lz[z] = l_sum[...] + l_y[...]
    gz[z] = (gfull[c, own] + g_in[own] + gy_in[...].astype(F32)).astype(BF16)

    def gz_copy(k, slot):
        return remote(gz.at[slot], gz.at[slot], gz_s.at[k], gz_r.at[slot], dev((z + k) % Z, y, c))

    def lz_copy(k, slot):
        return remote(lz.at[slot], lz.at[slot], lz_s.at[k], lz_r.at[slot], dev((z + k) % Z, y, c))

    def gz_start(k, carry):
        gz_copy(k, z).start()
        lz_copy(k, z).start()
        return carry

    lax.fori_loop(1, Z, gz_start, 0)

    lax.fori_loop(1, Z, z_step, 0)

    def gz_wait(k, carry):
        slot = (z + k) % Z
        gz_copy(k, slot).wait_recv()
        lz_copy(k, slot).wait_recv()
        return carry

    lax.fori_loop(1, Z, gz_wait, 0)
    g_total, l_total = gz[0].astype(F32), lz[0]
    for k in range(1, Z):
        g_total = g_total + gz[k].astype(F32)
        l_total = l_total + lz[k]
    gh[y] = g_total.astype(BF16)
    ex_gh = remote(gh.at[y], gh.at[y], ex_s.at[5], ex_r.at[5], y_peer)
    ex_gh.start()
    loss_ref[...] = l_total / F32(Z * 4 * rows)

    lax.fori_loop(2 * Z - 2, 2 * Z, y_step, 0)
    lax.fori_loop(Z, 2 * Z - 2, z_step, 0)

    remote(gh.at[1 - y], gh.at[1 - y], ex_s.at[5], ex_r.at[5], y_peer).wait_recv()
    ex_gp = remote(gh, gp, ex_s.at[6], ex_r.at[6], core_peer)
    ex_gp.start()

    lax.fori_loop(2 * Z - 2, 2 * Z, z_step, 0)

    gn32[...] = lax.dot_general(
        dpre[...], ws[...], (((1,), (1,)), ((), ())), preferred_element_type=F32
    )
    ex_gp.wait_recv()
    for h in range(2):
        grads_ref[c, h * half : (h + 1) * half] = gh[h]
        grads_ref[1 - c, h * half : (h + 1) * half] = gp[h]

    for h in range(2):
        @pl.when(z > 0)
        def _():
            up_copy(2 * z + h).wait_recv()
            town[h] += up_in[2 * z + h].astype(F32)

        @pl.when(z < Z - 1)
        def _():
            dn_copy(2 * z + h).wait_recv()
            town[h] += dn_in[2 * z + h].astype(F32)

        at_half = slice(h * half, (h + 1) * half)
        gfeat_ref[:, at_half] = gn32[:, at_half] + jnp.transpose(town[h])

    def sent(zs, carry):
        for h in range(2):
            @pl.when((zs <= z) & (z < Z - 1))
            def _():
                go_up(zs, h).wait_send()

            @pl.when((zs >= z) & (z > 0))
            def _():
                go_dn(zs, h).wait_send()

            go_y(zs, h).wait_send()
            go_core(zs, 0, h).wait_send()
            go_core(zs, 1, h).wait_send()
            y_copy(2 * zs + h).wait_send()

            @pl.when(zs != z)
            def _():
                up_copy(2 * zs + h).wait_send()

        return carry

    lax.fori_loop(0, Z, sent, 0)

    def sent_z(k, carry):
        gz_copy(k, z).wait_send()
        lz_copy(k, z).wait_send()
        return carry

    lax.fori_loop(1, Z, sent_z, 0)
    for copy in (adj_swap, ex_gn, ex_l, ex_g, ex_ly, ex_gy, ex_gh, ex_gp):
        copy.wait_send()


def finish_kernel(loss_ref, grads_ref, gfeat_ref, loss_out, gself_out, gneigh_out, gfeat_out):
    loss_out[0] = loss_ref[0, 0]
    gself_out[...] = grads_ref[0].astype(F32)
    gneigh_out[...] = grads_ref[1].astype(F32)
    gfeat_out[...] = gfeat_ref[...]


def on_device(
    features, self_weight, neigh_weight, tile_vals, tile_cols, tile_count, pos_index, neg_index
):
    rows, width = features.shape
    shards = lax.axis_size("row")
    Z = shards // 4
    adj, degree = dense_rows(tile_vals, tile_cols, tile_count, shards)
    adj = adj.reshape(shards // 2, 2, rows, rows)
    vmem = pl.BlockSpec(memory_space=pltpu.VMEM)
    anywhere = pl.BlockSpec(memory_space=pl.ANY)
    half = rows // 2
    dma = pltpu.SemaphoreType.DMA
    parts = pl.pallas_call(
        functools.partial(layer_kernel, Z),
        in_specs=[anywhere] * 3 + [vmem, anywhere, vmem, vmem],
        out_specs=[vmem] * 3,
        out_shape=[
            jax.ShapeDtypeStruct((8, 128), F32),
            jax.ShapeDtypeStruct((2, width, width), BF16),
            jax.ShapeDtypeStruct((rows, width), F32),
        ],
        scratch_shapes=[
            pltpu.VMEM((shards, rows, width), BF16),
            pltpu.VMEM((width, width), BF16),
            pltpu.VMEM((width, width), BF16),
            pltpu.VMEM((rows, 128), F32),
            pltpu.VMEM((shards // 2, rows, rows), BF16),
            pltpu.VMEM((2 * rows, 128), jnp.int32),
            pltpu.VMEM((3 * rows, width), F32),
            pltpu.VMEM((rows, width), BF16),
            pltpu.VMEM((rows, width), BF16),
            pltpu.VMEM((2, width, rows), BF16),
            pltpu.VMEM((rows, width), F32),
            pltpu.VMEM((2, width, width), F32),
            pltpu.VMEM((width, width), F32),
            pltpu.VMEM((half, width), BF16),
            pltpu.VMEM((half, width), BF16),
            pltpu.VMEM((Z, half, width), BF16),
            pltpu.VMEM((2, half, width), BF16),
            pltpu.VMEM((2, half, width), BF16),
            pltpu.VMEM((8, 128), F32),
            pltpu.VMEM((8, 128), F32),
            pltpu.VMEM((8, 128), F32),
            pltpu.VMEM((8, 128), F32),
            pltpu.VMEM((Z, 8, 128), F32),
            pltpu.VMEM((2 * Z, half, rows), BF16),
            pltpu.VMEM((2 * Z, half, rows), BF16),
            pltpu.VMEM((2 * Z, half, rows), BF16),
            pltpu.VMEM((2 * Z, half, rows), BF16),
            pltpu.VMEM((2 * Z, half, rows), BF16),
            pltpu.VMEM((half, rows), F32),
            pltpu.VMEM((2, half, rows), F32),
            dma((4,)), dma(()), dma(()), dma((2 * shards,)), dma((2 * Z,)), dma((2 * Z,)),
            dma((2 * Z,)), dma((4 * Z,)), dma((7,)), dma((7,)), dma((Z,)), dma((Z,)), dma((Z,)),
            dma((Z,)), dma((2 * Z,)), dma((2 * Z,)), dma((2 * Z,)), dma((2 * Z,)), dma((2 * Z,)),
        ],
        compiler_params=pltpu.CompilerParams(
            collective_id=0, has_side_effects=True,
            vmem_limit_bytes=8 * 1024 * 1024 + shards * rows * rows * 2 * 5,
        ),
    )(
        features, self_weight, neigh_weight, adj, degree,
        pos_index.reshape(1, rows), neg_index.reshape(1, rows),
    )
    square = jax.ShapeDtypeStruct((width, width), F32)
    return pl.pallas_call(
        finish_kernel,
        in_specs=[vmem] * 3,
        out_specs=[pl.BlockSpec(memory_space=pltpu.SMEM)] + [vmem] * 3,
        out_shape=[
            jax.ShapeDtypeStruct((1,), F32), square, square,
            jax.ShapeDtypeStruct((rows, width), F32),
        ],
    )(*parts)


def solution(mesh):
    placed = (
        P(("groups", "row"), None),
        P(),
        P(),
        P(("groups", "row"), None, None, None),
        P(("groups", "row"), None),
        P(("groups", "row")),
        P(("groups", "row")),
        P(("groups", "row")),
    )
    return jax.shard_map(
        on_device,
        mesh=mesh,
        in_specs=placed,
        out_specs=(P("groups"), P("groups", None), P("groups", None), P(("groups", "row"), None)),
        check_vma=False,
    )
```
